32 devices in a mesh: section: 4 (over y, x), tx: 4 (over z), ty: 2 (over core).
Axes of the slice: x: 2, y: 2, z: 4, core: 2. Of those that a mesh axis runs over, the one named last changes fastest.
Arguments:
- frames: bfloat16 [2, 32, 32, 256], P(None, None, 'tx', 'ty'), may hold values from -6 to 6
- h_init: bfloat16 [4, 32, 32, 256], P('section', None, 'tx', 'ty'), may hold values from -3 to 3
- c_init: float32 [4, 32, 32, 256], P('section', None, 'tx', 'ty'), may hold values from -6 to 6
- weights: bfloat16 [4, 576, 128], P('section'), may hold values from -0.25 to 0.25
- biases: float32 [4, 128], P('section'), may hold values from -3 to 3
- cotangent: bfloat16 [2, 32, 32, 256], P(None, None, 'tx', 'ty'), may hold values from -6 to 6
Outputs:
- hiddens: bfloat16 [4, 2, 32, 32, 256], P('section', None, None, 'tx', 'ty')
- grad_weights: float32 [4, 576, 128], P('section')
- grad_biases: float32 [4, 128], P('section')
The draws below stay inside these ranges and needn't reach their ends.
All inputs are finite; a program needn't handle non-finite values.
Results may differ from the reference program's by a relative error of at most 0.0035.
Values may be sent and summed in bfloat16 or wider, within the bound.
A program may use at most 64 MiB of HBM per device.

```python
import jax
import jax.numpy as jnp

HID = 32
FRAMES = 2
SECTIONS = 4
NX = 32
NY = 256


def block_scale(key, shape, cuts, smallest, largest):
    level, own = 1.0, jax.random.fold_in(key, 6)
    for axis_at, blocks in cuts:
        heights = jnp.exp(jax.random.uniform(jax.random.fold_in(own, axis_at), (blocks,), jnp.float32, smallest / len(cuts), largest / len(cuts)))
        level = level * jnp.repeat(heights, shape[axis_at] // blocks).reshape([-1 if axis == axis_at else 1 for axis in range(len(shape))])
    return level


def normal_values(key, shape, scale, reach, cuts=(), dtype=jnp.bfloat16):
    factor_of = block_scale(key, shape, cuts, -0.22, 0.18) if cuts else 1.0
    result = jax.random.normal(key, shape, jnp.float32) * scale * factor_of
    return jnp.minimum(jnp.maximum(result, -reach), reach).astype(dtype)


def setup_inputs(seed: int = 0) -> dict:
    arg_keys = jax.random.split(jax.random.key(seed), 7)
    frames = normal_values(arg_keys[0], (FRAMES, HID, NX, NY), 1.0, 6.0, ((2, 4), (3, 2)))
    h_init = normal_values(arg_keys[1], (SECTIONS, HID, NX, NY), 0.5, 3.0, ((0, 4), (2, 4), (3, 2)))
    c_init = normal_values(arg_keys[2], (SECTIONS, HID, NX, NY), 1.0, 6.0, ((0, 4), (2, 4), (3, 2)), jnp.float32)
    weights = normal_values(arg_keys[3], (SECTIONS, 18 * HID, 4 * HID), (18 * HID) ** -0.5, 0.25, ((0, 4),))
    biases = normal_values(arg_keys[4], (SECTIONS, 4 * HID), 0.5, 3.0, ((0, 4),), jnp.float32)
    cotangent = normal_values(arg_keys[5], (FRAMES, HID, NX, NY), 1.0, 6.0, ((2, 4), (3, 2)))
    return dict(frames=frames, h_init=h_init, c_init=c_init, weights=weights, biases=biases, cotangent=cotangent)


def unfold_cells(padded, row_count, col_count):
    pieces = [padded[:, offset_row:offset_row + row_count, offset_col:offset_col + col_count] for offset_row in range(3) for offset_col in range(3)]
    stacked = jnp.concatenate(pieces, 0)
    return stacked.reshape(stacked.shape[0], row_count * col_count)


def cell_update(gates, c_before, row_count, col_count):
    width = gates.shape[0] // 4
    shaped = gates.reshape(4, width, row_count, col_count)
    gate_in = jax.nn.sigmoid(shaped[0])
    gate_forget = jax.nn.sigmoid(shaped[1])
    gate_out = jax.nn.sigmoid(shaped[2])
    gate_cell = jnp.tanh(shaped[3])
    c_after = gate_forget * c_before + gate_in * gate_cell
    h_after = (gate_out * jnp.tanh(c_after)).astype(jnp.bfloat16)
    return h_after, c_after, jnp.stack([gate_in, gate_forget, gate_out, gate_cell])


def gate_grads(activity, c_before, c_after, dh_total, dc_incoming):
    gate_in = activity[0]
    gate_forget = activity[1]
    gate_out = activity[2]
    gate_cell = activity[3]
    squash = jnp.tanh(c_after)
    dc_total = dc_incoming + dh_total * gate_out * (1.0 - squash * squash)
    delta = jnp.concatenate([
        dc_total * gate_cell * gate_in * (1.0 - gate_in),
        dc_total * c_before * gate_forget * (1.0 - gate_forget),
        dh_total * squash * gate_out * (1.0 - gate_out),
        dc_total * gate_in * (1.0 - gate_cell * gate_cell)], 0).astype(jnp.bfloat16)
    return delta, dc_total * gate_forget


def flipped_weight(weight):
    inner = weight.shape[0] // 9
    outer = weight.shape[1]
    return weight.reshape(9, inner, outer)[::-1].transpose(1, 0, 2).reshape(inner, 9 * outer)


def reference(frames, h_init, c_init, weights, biases, cotangent):
    section_total = weights.shape[0]
    frame_count = frames.shape[0]
    width = h_init.shape[1]
    row_count = frames.shape[2]
    col_count = frames.shape[3]
    border = ((0, 0), (1, 1), (1, 1))
    layer_inputs = [frames[index] for index in range(frame_count)]
    records = []
    hiddens = []
    for layer in range(section_total):
        h_now = h_init[layer]
        c_now = c_init[layer]
        record = []
        outputs = []
        for frame in range(frame_count):
            joined = jnp.concatenate([layer_inputs[frame], h_now], 0)
            padded = jnp.pad(joined, border)
            patches = unfold_cells(padded, row_count, col_count)
            gates = jnp.dot(weights[layer].T, patches, preferred_element_type=jnp.float32) + biases[layer][:, None]
            h_next, c_next, activity = cell_update(gates, c_now, row_count, col_count)
            record.append((padded, activity, c_now, c_next))
            h_now, c_now = h_next, c_next
            outputs.append(h_next)
        records.append(record)
        hiddens.append(jnp.stack(outputs))
        layer_inputs = outputs
    upstream = [cotangent[index] for index in range(frame_count)]
    grad_w = [None] * section_total
    grad_b = [None] * section_total
    for layer in reversed(range(section_total)):
        flipped = flipped_weight(weights[layer])
        dh_carry = jnp.zeros((width, row_count, col_count), jnp.float32)
        dc_carry = jnp.zeros((width, row_count, col_count), jnp.float32)
        w_total = jnp.zeros(weights.shape[1:], jnp.float32)
        b_total = jnp.zeros((weights.shape[2],), jnp.float32)
        below = [None] * frame_count
        for frame in reversed(range(frame_count)):
            padded, activity, c_before, c_after = records[layer][frame]
            dh_total = upstream[frame].astype(jnp.float32) + dh_carry
            delta, dc_carry = gate_grads(activity, c_before, c_after, dh_total, dc_carry)
            flat = delta.reshape(delta.shape[0], row_count * col_count)
            patches = unfold_cells(padded, row_count, col_count)
            w_total = w_total + jnp.dot(patches, flat.T, preferred_element_type=jnp.float32)
            b_total = b_total + jnp.sum(flat.astype(jnp.float32), axis=1)
            delta_pad = jnp.pad(delta, border)
            grad_z = jnp.dot(flipped, unfold_cells(delta_pad, row_count, col_count), preferred_element_type=jnp.float32)
            grad_z = grad_z.reshape(2 * width, row_count, col_count)
            below[frame] = grad_z[:width].astype(jnp.bfloat16)
            dh_carry = grad_z[width:]
        grad_w[layer] = w_total
        grad_b[layer] = b_total
        upstream = below
    return jnp.stack(hiddens), jnp.stack(grad_w), jnp.stack(grad_b)
```

```python
import functools

import jax
import jax.numpy as jnp
from jax import lax
from jax.experimental import pallas as pl
from jax.experimental.pallas import tpu as pltpu
from jax.sharding import PartitionSpec as P

MESH = pl.DeviceIdType.MESH
SIDES = [(-1, 0), (1, 0), (0, -1), (0, 1), (-1, -1), (-1, 1), (1, -1), (1, 1)]
SLOT = {side: index for index, side in enumerate(SIDES)}
F32 = jnp.float32
BF16 = jnp.bfloat16


def sigmoid(x):
    return 0.5 * jnp.tanh(0.5 * x) + 0.5


def dot(x, y, contract):
    return lax.dot_general(x, y, (contract, ((), ())), preferred_element_type=F32)


def kernel(dims, frames, h_init, c_init, weight, bias, cotangent, hidden, grad_w, grad_b,
           wt, wb, bcol, zz, dd, coef, cell, x_in, dx_in, dx_out, da, dh_carry, dc_carry,
           pack, halo, d_pack, d_halo, total, recv1, part1, recv2, done,
           h_send, h_recv, x_send, x_recv, d_send, d_recv, u_send, u_recv,
           s1, r1, s2, r2, s3, r3, s4, r4):
    sections, m, n = dims
    frame_count, width, cells = frames.shape
    cols = 128
    rows = cells // cols
    gates = 4 * width
    taps = weight.shape[0] // 3
    sec = lax.axis_index("section")
    tx = lax.axis_index("tx")
    ty = lax.axis_index("ty")
    pending = []

    def present(a, b):
        ok = jnp.bool_(True)
        if a:
            ok = ok & (tx + a >= 0) & (tx + a < m)
        if b:
            ok = ok & (ty + b >= 0) & (ty + b < n)
        return ok

    def start(cond, src, dst, send_sem, recv_sem, device):
        def make():
            return pltpu.make_async_remote_copy(
                src_ref=src, dst_ref=dst, send_sem=send_sem, recv_sem=recv_sem,
                device_id=device, device_id_type=MESH)

        @pl.when(cond)
        def _():
            make().start()

        pending.append((cond, make))

    def arrive(cond, dst, send_sem, recv_sem, device):
        @pl.when(cond)
        def _():
            pltpu.make_async_remote_copy(
                src_ref=dst, dst_ref=dst, send_sem=send_sem, recv_sem=recv_sem,
                device_id=device, device_id_type=MESH).wait_recv()

    def send_sides(cond, target, first, last, packs, dst, send_sems, recv_sems):
        for d, (a, b) in enumerate(SIDES):
            src = packs[(b + 1) // 2] if b else (first if a < 0 else last)
            slot = SLOT[(-a, -b)]
            start(cond & present(a, b), src, dst.at[slot], send_sems.at[d], recv_sems.at[slot],
                  (target, tx + a, ty + b))

    def wait_sides(source, dst, send_sems, recv_sems):
        for d, (a, b) in enumerate(SIDES):
            arrive(present(a, b), dst.at[d], send_sems.at[d], recv_sems.at[d],
                   (source, tx + a, ty + b))

    def packed(row_of, height):
        lane = lax.broadcasted_iota(jnp.int32, (height, cols), 1)
        low = jnp.zeros((height, cols), F32)
        high = jnp.zeros((height, cols), F32)
        for r in range(rows):
            value = row_of(r)
            low = jnp.where(lane == r, pltpu.roll(value, r, 1) if r else value, low)
            high = jnp.where(lane == r, pltpu.roll(value, r + 1, 1), high)
        return low.astype(BF16), high.astype(BF16)

    def row_slice(r):
        return pl.ds(r * cols, cols)

    def spread(row_of, sides, height, store):
        lane = lax.broadcasted_iota(jnp.int32, (height, cols), 1)
        side = {key: sides[SLOT[key]].astype(F32) for key in SIDES}
        for q in range(rows + 2):
            if q == 0:
                value, source, at = side[(-1, 0)], -1, rows - 1
            elif q == rows + 1:
                value, source, at = side[(1, 0)], 1, 0
            else:
                value, source, at = row_of(q - 1), 0, q - 1
            low = side[(source, -1)]
            high = side[(source, 1)]
            low = pltpu.roll(low, (cols - at) % cols, 1) if at else low
            high = pltpu.roll(high, cols - 1 - at, 1)
            store(0, q, jnp.where(lane == 0, low, pltpu.roll(value, 1, 1)).astype(BF16))
            store(1, q, value.astype(BF16))
            store(2, q, jnp.where(lane == cols - 1, high, pltpu.roll(value, cols - 1, 1)).astype(BF16))

    halo[...] = jnp.zeros_like(halo)
    d_halo[...] = jnp.zeros_like(d_halo)
    total[...] = jnp.zeros_like(total)

    @pl.when(sec == 0)
    def _():
        x_in[...] = frames[...]

    @pl.when(sec == sections - 1)
    def _():
        dx_in[...] = cotangent[...]

    barrier = pltpu.get_barrier_semaphore()
    count = jnp.int32(m - 1 + n - 1)

    def greet(cond, device):
        @pl.when(cond)
        def _():
            pl.semaphore_signal(barrier, inc=1, device_id=device, device_id_type=MESH)
        return jnp.where(cond, 1, 0).astype(jnp.int32)

    for j in range(m):
        greet(tx != j, (sec, j, ty))
    for j in range(n):
        greet(ty != j, (sec, tx, j))
    for a, b in SIDES:
        if a and b:
            count = count + greet(present(a, b), (sec, tx + a, ty + b))
    for step in (-1, 1):
        there = (sec + step >= 0) & (sec + step < sections)
        for a, b in [(0, 0)] + SIDES:
            count = count + greet(there & present(a, b), (sec + step, tx + a, ty + b))

    low, high = packed(lambda r: h_init[:, row_slice(r)].astype(F32), width)
    pack[0, 0] = low
    pack[0, 1] = high

    @pl.when(sec == 0)
    def _():
        for t in range(frame_count):
            low, high = packed(lambda r: frames[t, :, row_slice(r)].astype(F32), width)
            pack[1 + t, 0] = low
            pack[1 + t, 1] = high

    for kr in range(3):
        wt[kr] = weight[kr * taps:(kr + 1) * taps, :].astype(F32).T.astype(BF16)
        for kc in range(3):
            k = kr * 3 + kc
            wb[2 - kr, :, (2 - kc) * gates:(3 - kc) * gates] = weight[k * 2 * width:(k + 1) * 2 * width, :]
    bcol[...] = jnp.broadcast_to(bias[...], (gates, gates)).T
    dh_carry[...] = jnp.zeros_like(dh_carry)
    dc_carry[...] = jnp.zeros_like(dc_carry)
    cell[...] = c_init[...]

    pl.semaphore_wait(barrier, count)

    first, last = row_slice(0), row_slice(rows - 1)
    for t in range(frame_count):
        send_sides(sec == 0, sec, frames.at[t, :, first], frames.at[t, :, last],
                   (pack.at[1 + t, 0], pack.at[1 + t, 1]), halo.at[t],
                   h_send.at[1 + t], h_recv.at[t])
        if t == 0:
            send_sides(jnp.bool_(True), sec, h_init.at[:, first], h_init.at[:, last],
                       (pack.at[0, 0], pack.at[0, 1]), halo.at[frame_count],
                       h_send.at[0], h_recv.at[frame_count])

    for t in range(frame_count):
        slot = frame_count + t
        wait_sides(sec, halo.at[slot], h_send.at[0], h_recv.at[slot])
        prior = h_init if t == 0 else hidden.at[t - 1]

        def store_h(kc, q, value):
            zz[t, kc * 2 * width + width:(kc + 1) * 2 * width, row_slice(q)] = value

        def store_x(kc, q, value):
            zz[t, kc * 2 * width:kc * 2 * width + width, row_slice(q)] = value

        spread(lambda r: prior[:, row_slice(r)].astype(F32), halo[slot], width, store_h)
        arrive(sec > 0, x_in.at[t], x_send.at[t], x_recv.at[t], (jnp.maximum(sec - 1, 0), tx, ty))
        wait_sides(jnp.maximum(sec - 1, 0), halo.at[t], h_send.at[0], h_recv.at[t])
        spread(lambda r: x_in[t, :, row_slice(r)].astype(F32), halo[t], width, store_x)

        act = jnp.zeros((gates, cells), F32)
        for kr in range(3):
            act = act + dot(wt[kr], zz[t, :, kr * cols:kr * cols + cells], ((1,), (0,)))
        column = bcol[...]
        h_rows = []
        for r in range(rows):
            at = row_slice(r)
            a = act[:, r * cols:(r + 1) * cols] + column
            gate_in = sigmoid(a[:width])
            gate_forget = sigmoid(a[width:2 * width])
            gate_out = sigmoid(a[2 * width:3 * width])
            gate_cell = jnp.tanh(a[3 * width:])
            before = cell[:, at]
            after = gate_forget * before + gate_in * gate_cell
            squash = jnp.tanh(after)
            h = gate_out * squash
            cell[:, at] = after
            hidden[t, :, at] = h.astype(BF16)
            h_rows.append(h)
            coef[t, 0, :, at] = gate_cell * gate_in * (1.0 - gate_in)
            coef[t, 1, :, at] = before * gate_forget * (1.0 - gate_forget)
            coef[t, 2, :, at] = squash * gate_out * (1.0 - gate_out)
            coef[t, 3, :, at] = gate_in * (1.0 - gate_cell * gate_cell)
            coef[t, 4, :, at] = gate_out * (1.0 - squash * squash)
            coef[t, 5, :, at] = gate_forget
        start(sec < sections - 1, hidden.at[t], x_in.at[t], x_send.at[t], x_recv.at[t],
              (sec + 1, tx, ty))
        slot = 1 + frame_count + t
        low, high = packed(lambda r: h_rows[r], width)
        pack[slot, 0] = low
        pack[slot, 1] = high
        sides = (hidden.at[t, :, first], hidden.at[t, :, last], (pack.at[slot, 0], pack.at[slot, 1]))
        send_sides(sec < sections - 1, sec + 1, *sides, halo.at[t],
                   h_send.at[1 + 2 * frame_count + t], h_recv.at[t])
        if t < frame_count - 1:
            send_sides(jnp.bool_(True), sec, *sides, halo.at[slot], h_send.at[slot], h_recv.at[slot])

    for t in reversed(range(frame_count)):
        arrive(sec < sections - 1, dx_in.at[t], u_send.at[t], u_recv.at[t],
               (jnp.minimum(sec + 1, sections - 1), tx, ty))
        da_rows = []
        for r in range(rows):
            at = row_slice(r)
            dh = dx_in[t, :, at].astype(F32) + dh_carry[:, at]
            dc = dc_carry[:, at] + dh * coef[t, 4, :, at]
            dc_carry[:, at] = dc * coef[t, 5, :, at]
            row = jnp.concatenate([dc * coef[t, 0, :, at], dc * coef[t, 1, :, at],
                                   dh * coef[t, 2, :, at], dc * coef[t, 3, :, at]], 0)
            da[t, :, at] = row.astype(BF16)
            da_rows.append(row)
        low, high = packed(lambda r: da_rows[r], gates)
        d_pack[t, 0] = low
        d_pack[t, 1] = high
        below = jnp.bool_(True) if t else sec > 0
        send_sides(below, sec, da.at[t, :, first], da.at[t, :, last],
                   (d_pack.at[t, 0], d_pack.at[t, 1]), d_halo.at[t], d_send.at[t], d_recv.at[t])
        for kr in range(3):
            at = pl.ds(kr * taps, taps)
            total[at, :] += dot(zz[t, :, kr * cols:kr * cols + cells], da[t], ((1,), (1,)))
        total[pl.ds(3 * taps, 8), :] += dot(jnp.ones((8, cells), BF16), da[t], ((1,), (1,)))

        def input_grad():
            wait_sides(sec, d_halo.at[t], d_send.at[t], d_recv.at[t])

            def store_d(kc, q, value):
                dd[kc * gates:(kc + 1) * gates, row_slice(q)] = value

            spread(lambda r: da[t, :, row_slice(r)].astype(F32), d_halo[t], gates, store_d)
            dz = jnp.zeros((2 * width, cells), F32)
            for kr in range(3):
                dz = dz + dot(wb[kr], dd[:, kr * cols:kr * cols + cells], ((1,), (0,)))
            dx_out[t] = dz[:width].astype(BF16)
            if t:
                dh_carry[...] = dz[width:]

        if t:
            input_grad()
        else:
            pl.when(sec > 0)(input_grad)
        start(sec > 0, dx_out.at[t], dx_in.at[t], u_send.at[t], u_recv.at[t], (sec - 1, tx, ty))

    c1 = total.shape[0] // n
    c2 = c1 // m
    for j in range(n):
        start(ty != j, total.at[pl.ds(j * c1, c1)], recv1.at[ty], s1.at[j], r1.at[ty], (sec, tx, j))
    mine1 = pl.ds(pl.multiple_of(ty * c1, 16), c1)
    part1[...] = total[mine1, :]
    for j in range(n):
        arrive(ty != j, recv1.at[j], s1.at[j], r1.at[j], (sec, tx, j))

        @pl.when(ty != j)
        def _():
            part1[...] += recv1[j]
    for j in range(m):
        start(tx != j, part1.at[pl.ds(j * c2, c2)], recv2.at[tx], s2.at[j], r2.at[tx], (sec, j, ty))
    mine2 = pl.ds(pl.multiple_of(tx * c2, 16), c2)
    for j in range(m):
        arrive(tx != j, recv2.at[j], s2.at[j], r2.at[j], (sec, j, ty))

        @pl.when(tx != j)
        def _():
            part1[mine2, :] += recv2[j]
    own = pl.ds(pl.multiple_of(ty * c1 + tx * c2, 16), c2)
    done[own, :] = part1[mine2, :].astype(BF16)
    for j in range(m):
        start(tx != j, done.at[own], done.at[own], s3.at[j], r3.at[tx], (sec, j, ty))
    for j in range(m):
        theirs = pl.ds(pl.multiple_of(ty * c1 + j * c2, 16), c2)
        arrive(tx != j, done.at[theirs], s3.at[j], r3.at[j], (sec, j, ty))
    for j in range(n):
        start(ty != j, done.at[mine1], done.at[mine1], s4.at[j], r4.at[ty], (sec, tx, j))
    for j in range(n):
        arrive(ty != j, done.at[pl.ds(j * c1, c1)], s4.at[j], r4.at[j], (sec, tx, j))
    grad_w[...] = done[pl.ds(0, 3 * taps), :].astype(F32)
    grad_b[...] = done[pl.ds(3 * taps, 16), :].astype(F32)[0:1]

    for cond, make in pending:
        pl.when(cond)(lambda make=make: make().wait_send())


def body(dims, frames, h_init, c_init, weights, biases, cotangent):
    sections, m, n = dims
    frame_count, width, row_count, col_count = frames.shape
    cells = row_count * col_count
    ext = cells + 2 * col_count
    gates = 4 * width
    taps = weights.shape[1] // 3
    unit = m * n * 16
    tall = -(-(3 * taps + 8) // unit) * unit
    c1 = tall // n
    c2 = c1 // m
    vmem = pl.BlockSpec(memory_space=pltpu.VMEM)
    dma = pltpu.SemaphoreType.DMA
    f = frame_count
    scratch = [
        pltpu.VMEM((3, gates, taps), BF16),
        pltpu.VMEM((3, 2 * width, 3 * gates), BF16),
        pltpu.VMEM((gates, gates), F32),
        pltpu.VMEM((f, taps, ext), BF16),
        pltpu.VMEM((3 * gates, ext), BF16),
        pltpu.VMEM((f, 6, width, cells), F32),
        pltpu.VMEM((width, cells), F32),
        pltpu.VMEM((f, width, cells), BF16),
        pltpu.VMEM((f, width, cells), BF16),
        pltpu.VMEM((f, width, cells), BF16),
        pltpu.VMEM((f, gates, cells), BF16),
        pltpu.VMEM((width, cells), F32),
        pltpu.VMEM((width, cells), F32),
        pltpu.VMEM((1 + 2 * f, 2, width, col_count), BF16),
        pltpu.VMEM((2 * f, 8, width, col_count), BF16),
        pltpu.VMEM((f, 2, gates, col_count), BF16),
        pltpu.VMEM((f, 8, gates, col_count), BF16),
        pltpu.VMEM((tall, gates), F32),
        pltpu.VMEM((n, c1, gates), F32),
        pltpu.VMEM((c1, gates), F32),
        pltpu.VMEM((m, c2, gates), F32),
        pltpu.VMEM((tall, gates), BF16),
        dma((1 + 3 * f, 8)), dma((2 * f, 8)),
        dma((f,)), dma((f,)),
        dma((f, 8)), dma((f, 8)),
        dma((f,)), dma((f,)),
        dma((n,)), dma((n,)), dma((m,)), dma((m,)),
        dma((m,)), dma((m,)), dma((n,)), dma((n,)),
    ]
    hidden, grad_w, grad_b = pl.pallas_call(
        functools.partial(kernel, dims),
        out_shape=(
            jax.ShapeDtypeStruct((f, width, cells), BF16),
            jax.ShapeDtypeStruct((3 * taps, gates), F32),
            jax.ShapeDtypeStruct((1, gates), F32),
        ),
        in_specs=[vmem] * 6,
        out_specs=(vmem, vmem, vmem),
        scratch_shapes=scratch,
        compiler_params=pltpu.CompilerParams(
            collective_id=0, has_side_effects=True, vmem_limit_bytes=48 * 1024 * 1024),
    )(
        frames.reshape(f, width, cells),
        h_init.reshape(width, cells),
        c_init.reshape(width, cells),
        weights[0],
        biases,
        cotangent.reshape(f, width, cells),
    )
    return (hidden.reshape(1, f, width, row_count, col_count), grad_w[None], grad_b)


def solution(mesh):
    dims = (mesh.shape["section"], mesh.shape["tx"], mesh.shape["ty"])
    in_specs = (
        P(None, None, "tx", "ty"),
        P("section", None, "tx", "ty"),
        P("section", None, "tx", "ty"),
        P("section", None, None),
        P("section", None),
        P(None, None, "tx", "ty"),
    )
    out_specs = (P("section", None, None, "tx", "ty"), P("section", None, None), P("section", None))
    return jax.shard_map(functools.partial(body, dims), mesh=mesh, in_specs=in_specs,
                         out_specs=out_specs, check_vma=False)
```

```python
import functools

import jax
import jax.numpy as jnp
from jax import lax
from jax.experimental import pallas as pl
from jax.experimental.pallas import tpu as pltpu
from jax.sharding import PartitionSpec as P

MESH = pl.DeviceIdType.MESH
SIDES = [(-1, 0), (1, 0), (-1, -1), (0, -1), (1, -1), (-1, 1), (0, 1), (1, 1)]
SLOT = {side: index for index, side in enumerate(SIDES)}
F32 = jnp.float32
BF16 = jnp.bfloat16


def sigmoid(x):
    return 0.5 * jnp.tanh(0.5 * x) + 0.5


def dot(x, y, contract):
    return lax.dot_general(x, y, (contract, ((), ())), preferred_element_type=F32)


def kernel(dims, frames, h_init, c_init, weight, bias, cotangent, hidden, grad_w, grad_b,
           wt, wb, bcol, pick, place, zz, dd, coef, coef_b, coef_s, cell, x_in, dx_in, dx_out, dh_out, da,
           dh_e, dh_s, dc_e, dc_s, pack, row_in, col_in, c_pack, c_row_in, c_col_in,
           total, recv1, part1, recv2, done,
           h_send, h_recv, x_send, x_recv, c_send, c_recv, u_send, u_recv,
           s1, r1, s2, r2, s3, r3, s4, r4):
    sections, m, n = dims
    frame_count, width, cells = frames.shape
    cols = 128
    rows = cells // cols
    gates = 4 * width
    taps = weight.shape[0] // 3
    sec = lax.axis_index("section")
    tx = lax.axis_index("tx")
    ty = lax.axis_index("ty")
    pending = []
    always = jnp.bool_(True)

    def present(a, b):
        ok = always
        if a:
            ok = ok & (tx + a >= 0) & (tx + a < m)
        if b:
            ok = ok & (ty + b >= 0) & (ty + b < n)
        return ok

    def start(cond, src, dst, send_sem, recv_sem, device):
        def make():
            return pltpu.make_async_remote_copy(
                src_ref=src, dst_ref=dst, send_sem=send_sem, recv_sem=recv_sem,
                device_id=device, device_id_type=MESH)

        @pl.when(cond)
        def _():
            make().start()

        pending.append((cond, make))

    def arrive(cond, dst, send_sem, recv_sem, device):
        @pl.when(cond)
        def _():
            pltpu.make_async_remote_copy(
                src_ref=dst, dst_ref=dst, send_sem=send_sem, recv_sem=recv_sem,
                device_id=device, device_id_type=MESH).wait_recv()

    def landing(rows_ref, cols_ref, slot):
        return rows_ref.at[slot] if slot < 2 else cols_ref.at[slot - 2]

    def send_sides(cond, target, first, last, packed, rows_ref, cols_ref, send_sems, recv_sems):
        for d, (a, b) in enumerate(SIDES):
            src = packed if b else (first if a < 0 else last)
            slot = SLOT[(-a, -b)]
            start(cond & present(a, b), src, landing(rows_ref, cols_ref, slot), send_sems.at[d],
                  recv_sems.at[slot], (target, tx + a, ty + b))

    def wait_sides(source, rows_ref, cols_ref, send_sems, recv_sems):
        for d, (a, b) in enumerate(SIDES):
            arrive(present(a, b), landing(rows_ref, cols_ref, d), send_sems.at[d], recv_sems.at[d],
                   (source, tx + a, ty + b))

    def packed(tile):
        return dot(pick[...], tile, ((1,), (1,))).astype(BF16)

    def side_image(slots, height):
        return dot(slots.reshape(6 * 16, slots.shape[2])[:, :height], place[...], ((0,), (0,)))

    def row_slice(r):
        return pl.ds(r * cols, cols)

    lane = lax.broadcasted_iota(jnp.int32, (width, cols), 1)
    lane_d = lax.broadcasted_iota(jnp.int32, (gates, cols), 1)

    def spread(value, side, lanes, store):
        low = jnp.where(lanes == 0, side, pltpu.roll(value, 1, 1))
        high = jnp.where(lanes == cols - 1, side, pltpu.roll(value, cols - 1, 1))
        store(0, low.astype(BF16))
        store(1, value.astype(BF16))
        store(2, high.astype(BF16))

    row_in[...] = jnp.zeros_like(row_in)
    col_in[...] = jnp.zeros_like(col_in)
    c_row_in[...] = jnp.zeros_like(c_row_in)
    c_col_in[...] = jnp.zeros_like(c_col_in)

    @pl.when(sec == 0)
    def _():
        x_in[...] = frames[...]

    @pl.when(sec == sections - 1)
    def _():
        dx_in[...] = cotangent[...]

    barrier = pltpu.get_barrier_semaphore()
    count = jnp.int32(m - 1 + n - 1)

    def greet(cond, device):
        @pl.when(cond)
        def _():
            pl.semaphore_signal(barrier, inc=1, device_id=device, device_id_type=MESH)
        return jnp.where(cond, 1, 0).astype(jnp.int32)

    for j in range(m):
        greet(tx != j, (sec, j, ty))
    for j in range(n):
        greet(ty != j, (sec, tx, j))
    for a, b in SIDES:
        if a and b:
            count = count + greet(present(a, b), (sec, tx + a, ty + b))
    for step in (-1, 1):
        there = (sec + step >= 0) & (sec + step < sections)
        for a, b in [(0, 0)] + SIDES:
            count = count + greet(there & present(a, b), (sec + step, tx + a, ty + b))

    x_set, h_set, u_set, g_set = 0, frame_count, 2 * frame_count, 3 * frame_count
    total[...] = jnp.zeros_like(total)
    pack[...] = jnp.zeros_like(pack)
    c_pack[...] = jnp.zeros_like(c_pack)
    at_row = lax.broadcasted_iota(jnp.int32, (16, cells), 0)
    at_lane = lax.broadcasted_iota(jnp.int32, (16, cells), 1)
    spot = jnp.where(at_row < rows, at_row * cols, (at_row - rows) * cols + cols - 1)
    pick[...] = jnp.where(at_lane == spot, 1.0, 0.0).astype(BF16)
    r16 = lax.broadcasted_iota(jnp.int32, (16, cells + 2 * cols), 0)
    at_lane = lax.broadcasted_iota(jnp.int32, (16, cells + 2 * cols), 1)
    for k in range(6):
        r = r16 - rows if k < 3 else r16
        inside = (r >= 0) & (r < rows)
        edge = 0 if k < 3 else cols - 1
        if k % 3 == 0:
            spot = jnp.where(r == rows - 1, edge, -1)
        elif k % 3 == 1:
            spot = jnp.where(inside, (r + 1) * cols + edge, -1)
        else:
            spot = jnp.where(r == 0, (rows + 1) * cols + edge, -1)
        place[pl.ds(16 * k, 16), :] = jnp.where(at_lane == spot, 1.0, 0.0).astype(BF16)

    pack[h_set, :, 0:width] = packed(h_init[...])

    @pl.when(sec == 0)
    def _():
        for t in range(frame_count):
            pack[x_set + t, :, 0:width] = packed(frames[t])

    @pl.when(sec == sections - 1)
    def _():
        for t in range(frame_count):
            pack[u_set + t, :, 0:width] = packed(cotangent[t])

    for kr in range(3):
        wt[kr] = weight[kr * taps:(kr + 1) * taps, :].astype(F32).T.astype(BF16)
        for kc in range(3):
            k = kr * 3 + kc
            wb[2 - kr, :, (2 - kc) * gates:(3 - kc) * gates] = weight[k * 2 * width:(k + 1) * 2 * width, :]
    bcol[...] = jnp.broadcast_to(bias[...], (gates, gates)).T
    for ref in (dh_e, dh_s, dc_e, dc_s):
        ref[...] = jnp.zeros_like(ref)
    cell[...] = c_init[...]

    pl.semaphore_wait(barrier, count)

    first, last = row_slice(0), row_slice(rows - 1)

    def exchange(cond, target, tile, slot, to, event):
        send_sides(cond, target, tile.at[:, first], tile.at[:, last], pack.at[slot],
                   row_in.at[to], col_in.at[to], h_send.at[event], h_recv.at[to])

    def gathered(source, to):
        wait_sides(source, row_in.at[to], col_in.at[to], h_send.at[0], h_recv.at[to])

    extra = 4 * frame_count
    exchange(sec == 0, sec, frames.at[0], x_set, x_set, x_set)
    exchange(always, sec, h_init, h_set, h_set, h_set)
    for t in range(1, frame_count):
        exchange(sec == 0, sec, frames.at[t], x_set + t, x_set + t, x_set + t)
    for t in range(frame_count):
        exchange(sec == sections - 1, sec, cotangent.at[t], u_set + t, u_set + t, u_set + t)
    above = jnp.where(sec == sections - 1, sec, sec + 1)
    before_layer = jnp.where(sec == 0, sec, sec - 1)

    for t in range(frame_count):
        def store_z(offset, q):
            def store(kc, value):
                low = kc * 2 * width + offset
                zz[t, low:low + width, row_slice(q)] = value
            return store

        def fill(tile, to, offset):
            side = side_image(col_in[to], width)
            for q in range(rows + 2):
                if q == 0:
                    value = row_in[to, 0]
                elif q == rows + 1:
                    value = row_in[to, 1]
                else:
                    value = tile[:, row_slice(q - 1)]
                spread(value.astype(F32), side[:, q * cols:(q + 1) * cols], lane, store_z(offset, q))

        gathered(sec, h_set + t)
        fill(h_init if t == 0 else hidden.at[t - 1], h_set + t, width)
        arrive(sec > 0, x_in.at[t], x_send.at[t], x_recv.at[t], (before_layer, tx, ty))
        gathered(before_layer, x_set + t)
        fill(x_in.at[t], x_set + t, 0)

        act = jnp.zeros((gates, cells), F32)
        for kr in range(3):
            act = act + dot(wt[kr], zz[t, :, kr * cols:kr * cols + cells], ((1,), (0,)))
        column = bcol[...]
        for r in range(rows):
            at = row_slice(r)
            a = act[:, r * cols:(r + 1) * cols] + column
            gate_in = sigmoid(a[:width])
            gate_forget = sigmoid(a[width:2 * width])
            gate_out = sigmoid(a[2 * width:3 * width])
            gate_cell = jnp.tanh(a[3 * width:])
            before = cell[:, at]
            after = gate_forget * before + gate_in * gate_cell
            squash = jnp.tanh(after)
            cell[:, at] = after
            hidden[t, :, at] = (gate_out * squash).astype(BF16)
            for k, value in enumerate((
                    gate_cell * gate_in * (1.0 - gate_in),
                    before * gate_forget * (1.0 - gate_forget),
                    squash * gate_out * (1.0 - gate_out),
                    gate_in * (1.0 - gate_cell * gate_cell),
                    gate_out * (1.0 - squash * squash),
                    gate_forget)):
                coef[t, k, :, at] = value
                coef_b[t, k * width:(k + 1) * width, at] = value.astype(BF16)
        start(sec < sections - 1, hidden.at[t], x_in.at[t], x_send.at[t], x_recv.at[t],
              (sec + 1, tx, ty))
        pack[extra + t, :, 0:width] = packed(hidden[t])
        exchange(sec < sections - 1, sec + 1, hidden.at[t], extra + t, x_set + t, extra + t)
        if t < frame_count - 1:
            exchange(always, sec, hidden.at[t], extra + t, h_set + t + 1, h_set + t + 1)
        c_pack[t, :, 0:6 * width] = packed(coef_b[t])
        send_sides(always, sec, coef_b.at[t, :, first], coef_b.at[t, :, last], c_pack.at[t],
                   c_row_in.at[t], c_col_in.at[t], c_send.at[t], c_recv.at[t])

    for t in reversed(range(frame_count)):
        wait_sides(sec, c_row_in.at[t], c_col_in.at[t], c_send.at[t], c_recv.at[t])
        coef_s[...] = side_image(c_col_in[t], 6 * width)
        if t < frame_count - 1:
            gathered(sec, g_set + t + 1)
            dh_s[...] = side_image(col_in[g_set + t + 1], width)
            dh_e[:, row_slice(0)] = row_in[g_set + t + 1, 0].astype(F32)
            dh_e[:, row_slice(rows + 1)] = row_in[g_set + t + 1, 1].astype(F32)
        arrive(sec < sections - 1, dx_in.at[t], u_send.at[t], u_recv.at[t], (above, tx, ty))
        gathered(above, u_set + t)
        u_s = side_image(col_in[u_set + t], width)

        def gate_grads(u, dh_ref, dc_ref, at, k_of):
            dh = u + dh_ref[:, at]
            dc = dc_ref[:, at] + dh * k_of(4)
            dc_ref[:, at] = dc * k_of(5)
            return jnp.concatenate([dc * k_of(0), dc * k_of(1), dh * k_of(2), dc * k_of(3)], 0)

        for q in range(rows + 2):
            at = row_slice(q)
            if 0 < q <= rows:
                u = dx_in[t, :, row_slice(q - 1)].astype(F32)
                main = gate_grads(u, dh_e, dc_e, at, lambda k: coef[t, k, :, row_slice(q - 1)])
                da[t, :, row_slice(q - 1)] = main.astype(BF16)
            else:
                end = 0 if q == 0 else 1
                u = row_in[u_set + t, end].astype(F32)
                main = gate_grads(u, dh_e, dc_e, at, lambda k: (
                    c_row_in[t, end, k * width:(k + 1) * width, :].astype(F32)))
            side = gate_grads(u_s[:, q * cols:(q + 1) * cols], dh_s, dc_s, at,
                              lambda k: coef_s[k * width:(k + 1) * width, at])

            def store_d(kc, value):
                dd[kc * gates:(kc + 1) * gates, at] = value

            spread(main, side, lane_d, store_d)

        def input_grad():
            dz = jnp.zeros((2 * width, cells), F32)
            for kr in range(3):
                dz = dz + dot(wb[kr], dd[:, kr * cols:kr * cols + cells], ((1,), (0,)))
            dx_out[t] = dz[:width].astype(BF16)
            if t:
                dh_out[t] = dz[width:].astype(BF16)
                dh_e[:, pl.ds(cols, cells)] = dz[width:]

        if t:
            input_grad()
        else:
            pl.when(sec > 0)(input_grad)
        start(sec > 0, dx_out.at[t], dx_in.at[t], u_send.at[t], u_recv.at[t], (sec - 1, tx, ty))

        @pl.when(sec > 0)
        def _():
            pack[extra + frame_count + t, :, 0:width] = packed(dx_out[t])

        exchange(sec > 0, sec - 1, dx_out.at[t], extra + frame_count + t, u_set + t,
                 extra + frame_count + t)
        if t:
            pack[g_set + t, :, 0:width] = packed(dh_out[t])
            exchange(always, sec, dh_out.at[t], g_set + t, g_set + t, g_set + t)
        for kr in range(3):
            at = pl.ds(kr * taps, taps)
            total[at, :] += dot(zz[t, :, kr * cols:kr * cols + cells], da[t], ((1,), (1,)))
        total[pl.ds(3 * taps, 8), :] += dot(jnp.ones((8, cells), BF16), da[t], ((1,), (1,)))

    c1 = total.shape[0] // n
    c2 = c1 // m
    for j in range(n):
        start(ty != j, total.at[pl.ds(j * c1, c1)], recv1.at[ty], s1.at[j], r1.at[ty], (sec, tx, j))
    mine1 = pl.ds(pl.multiple_of(ty * c1, 16), c1)
    part1[...] = total[mine1, :]
    for j in range(n):
        arrive(ty != j, recv1.at[j], s1.at[j], r1.at[j], (sec, tx, j))

        @pl.when(ty != j)
        def _():
            part1[...] += recv1[j]
    for j in range(m):
        start(tx != j, part1.at[pl.ds(j * c2, c2)], recv2.at[tx], s2.at[j], r2.at[tx], (sec, j, ty))
    mine2 = pl.ds(pl.multiple_of(tx * c2, 16), c2)
    for j in range(m):
        arrive(tx != j, recv2.at[j], s2.at[j], r2.at[j], (sec, j, ty))

        @pl.when(tx != j)
        def _():
            part1[mine2, :] += recv2[j]
    own = pl.ds(pl.multiple_of(ty * c1 + tx * c2, 16), c2)
    done[own, :] = part1[mine2, :].astype(BF16)
    for j in range(m):
        start(tx != j, done.at[own], done.at[own], s3.at[j], r3.at[tx], (sec, j, ty))
    for j in range(m):
        theirs = pl.ds(pl.multiple_of(ty * c1 + j * c2, 16), c2)
        arrive(tx != j, done.at[theirs], s3.at[j], r3.at[j], (sec, j, ty))
    for j in range(n):
        start(ty != j, done.at[mine1], done.at[mine1], s4.at[j], r4.at[ty], (sec, tx, j))
    for j in range(n):
        arrive(ty != j, done.at[pl.ds(j * c1, c1)], s4.at[j], r4.at[j], (sec, tx, j))
    grad_w[...] = done[pl.ds(0, 3 * taps), :].astype(F32)
    grad_b[...] = done[pl.ds(3 * taps, 16), :].astype(F32)[0:1]

    for cond, make in pending:
        pl.when(cond)(lambda make=make: make().wait_send())


def body(dims, frames, h_init, c_init, weights, biases, cotangent):
    sections, m, n = dims
    frame_count, width, row_count, col_count = frames.shape
    cells = row_count * col_count
    ext = cells + 2 * col_count
    gates = 4 * width
    taps = weights.shape[1] // 3
    unit = m * n * 16
    tall = -(-(3 * taps + 8) // unit) * unit
    c1 = tall // n
    c2 = c1 // m
    vmem = pl.BlockSpec(memory_space=pltpu.VMEM)
    dma = pltpu.SemaphoreType.DMA
    f = frame_count
    scratch = [
        pltpu.VMEM((3, gates, taps), BF16),
        pltpu.VMEM((3, 2 * width, 3 * gates), BF16),
        pltpu.VMEM((gates, gates), F32),
        pltpu.VMEM((16, cells), BF16),
        pltpu.VMEM((6 * 16, ext), BF16),
        pltpu.VMEM((f, taps, ext), BF16),
        pltpu.VMEM((3 * gates, ext), BF16),
        pltpu.VMEM((f, 6, width, cells), F32),
        pltpu.VMEM((f, 6 * width, cells), BF16),
        pltpu.VMEM((6 * width, ext), F32),
        pltpu.VMEM((width, cells), F32),
        pltpu.VMEM((f, width, cells), BF16),
        pltpu.VMEM((f, width, cells), BF16),
        pltpu.VMEM((f, width, cells), BF16),
        pltpu.VMEM((f, width, cells), BF16),
        pltpu.VMEM((f, gates, cells), BF16),
        pltpu.VMEM((width, ext), F32),
        pltpu.VMEM((width, ext), F32),
        pltpu.VMEM((width, ext), F32),
        pltpu.VMEM((width, ext), F32),
        pltpu.VMEM((6 * f, 16, col_count), BF16),
        pltpu.VMEM((4 * f, 2, width, col_count), BF16),
        pltpu.VMEM((4 * f, 6, 16, col_count), BF16),
        pltpu.VMEM((f, 16, 2 * col_count), BF16),
        pltpu.VMEM((f, 2, 6 * width, col_count), BF16),
        pltpu.VMEM((f, 6, 16, 2 * col_count), BF16),
        pltpu.VMEM((tall, gates), F32),
        pltpu.VMEM((n, c1, gates), F32),
        pltpu.VMEM((c1, gates), F32),
        pltpu.VMEM((m, c2, gates), F32),
        pltpu.VMEM((tall, gates), BF16),
        dma((6 * f, 8)), dma((4 * f, 8)),
        dma((f,)), dma((f,)),
        dma((f, 8)), dma((f, 8)),
        dma((f,)), dma((f,)),
        dma((n,)), dma((n,)), dma((m,)), dma((m,)),
        dma((m,)), dma((m,)), dma((n,)), dma((n,)),
    ]
    hidden, grad_w, grad_b = pl.pallas_call(
        functools.partial(kernel, dims),
        out_shape=(
            jax.ShapeDtypeStruct((f, width, cells), BF16),
            jax.ShapeDtypeStruct((3 * taps, gates), F32),
            jax.ShapeDtypeStruct((1, gates), F32),
        ),
        in_specs=[vmem] * 6,
        out_specs=(vmem, vmem, vmem),
        scratch_shapes=scratch,
        compiler_params=pltpu.CompilerParams(
            collective_id=0, has_side_effects=True, vmem_limit_bytes=48 * 1024 * 1024),
    )(
        frames.reshape(f, width, cells),
        h_init.reshape(width, cells),
        c_init.reshape(width, cells),
        weights[0],
        biases,
        cotangent.reshape(f, width, cells),
    )
    return (hidden.reshape(1, f, width, row_count, col_count), grad_w[None], grad_b)


def solution(mesh):
    dims = (mesh.shape["section"], mesh.shape["tx"], mesh.shape["ty"])
    in_specs = (
        P(None, None, "tx", "ty"),
        P("section", None, "tx", "ty"),
        P("section", None, "tx", "ty"),
        P("section", None, None),
        P("section", None),
        P(None, None, "tx", "ty"),
    )
    out_specs = (P("section", None, None, "tx", "ty"), P("section", None, None), P("section", None))
    return jax.shard_map(functools.partial(body, dims), mesh=mesh, in_specs=in_specs,
                         out_specs=out_specs, check_vma=False)
```

```python
import functools

import jax
import jax.numpy as jnp
from jax import lax
from jax.experimental import pallas as pl
from jax.experimental.pallas import tpu as pltpu
from jax.sharding import PartitionSpec as P

MESH = pl.DeviceIdType.MESH
SIDES = [(-1, 0), (1, 0), (-1, -1), (0, -1), (1, -1), (-1, 1), (0, 1), (1, 1)]
SLOT = {side: index for index, side in enumerate(SIDES)}
F32 = jnp.float32
BF16 = jnp.bfloat16


def sigmoid(x):
    return 0.5 * jnp.tanh(0.5 * x) + 0.5


def dot(x, y, contract):
    return lax.dot_general(x, y, (contract, ((), ())), preferred_element_type=F32)


def kernel(dims, frames, h_hbm, c_hbm, weight_hbm, bias_hbm, cotangent, hidden, grad_w, grad_b,
           weight, bias, raw, flat, h_init, wt, wb, bcol, pick, place, zz, dd, coef, coef_b, coef_s, cell, x_in, dx_in, dx_out, dh_out, da,
           dh_e, dh_s, dc_e, dc_s, pack, row_in, col_in, c_pack, c_row_in, c_col_in,
           total, recv1, part1, recv2, done,
           h_send, h_recv, x_send, x_recv, c_send, c_recv, u_send, u_recv,
           s1, r1, s2, r2, s3, r3, s4, r4, fetched):
    sections, m, n = dims
    frame_count, width, cells = hidden.shape
    cols = frames.shape[2]
    rows = cells // cols
    gates = 4 * width
    taps = weight.shape[0] // 3
    sec = lax.axis_index("section")
    tx = lax.axis_index("tx")
    ty = lax.axis_index("ty")
    pending = []
    always = jnp.bool_(True)

    def present(a, b):
        ok = always
        if a:
            ok = ok & (tx + a >= 0) & (tx + a < m)
        if b:
            ok = ok & (ty + b >= 0) & (ty + b < n)
        return ok

    def start(cond, src, dst, send_sem, recv_sem, device):
        def make():
            return pltpu.make_async_remote_copy(
                src_ref=src, dst_ref=dst, send_sem=send_sem, recv_sem=recv_sem,
                device_id=device, device_id_type=MESH)

        @pl.when(cond)
        def _():
            make().start()

        pending.append((cond, make))

    def arrive(cond, dst, send_sem, recv_sem, device):
        @pl.when(cond)
        def _():
            pltpu.make_async_remote_copy(
                src_ref=dst, dst_ref=dst, send_sem=send_sem, recv_sem=recv_sem,
                device_id=device, device_id_type=MESH).wait_recv()

    def landing(rows_ref, cols_ref, slot):
        return rows_ref.at[slot] if slot < 2 else cols_ref.at[slot - 2]

    def send_sides(cond, target, first, last, packed, rows_ref, cols_ref, send_sems, recv_sems,
                   which=range(8)):
        for d in which:
            a, b = SIDES[d]
            src = packed if b else (first if a < 0 else last)
            slot = SLOT[(-a, -b)]
            start(cond & present(a, b), src, landing(rows_ref, cols_ref, slot), send_sems.at[d],
                  recv_sems.at[slot], (target, tx + a, ty + b))

    def wait_sides(source, rows_ref, cols_ref, send_sems, recv_sems):
        for d, (a, b) in enumerate(SIDES):
            arrive(present(a, b), landing(rows_ref, cols_ref, d), send_sems.at[d], recv_sems.at[d],
                   (source, tx + a, ty + b))

    def packed(tile):
        return dot(pick[...], tile, ((1,), (1,))).astype(BF16)

    def side_image(slots, height):
        return dot(slots.reshape(6 * 16, slots.shape[2])[:, :height], place[...], ((0,), (0,)))

    def row_slice(r):
        return pl.ds(r * cols, cols)

    lane = lax.broadcasted_iota(jnp.int32, (width, cols), 1)
    lane_d = lax.broadcasted_iota(jnp.int32, (gates, cols), 1)

    def spread(value, side, lanes, store):
        low = jnp.where(lanes == 0, side, pltpu.roll(value, 1, 1))
        high = jnp.where(lanes == cols - 1, side, pltpu.roll(value, cols - 1, 1))
        store(0, low.astype(BF16))
        store(1, value.astype(BF16))
        store(2, high.astype(BF16))

    row_in[...] = jnp.zeros_like(row_in)
    col_in[...] = jnp.zeros_like(col_in)
    c_row_in[...] = jnp.zeros_like(c_row_in)
    c_col_in[...] = jnp.zeros_like(c_col_in)

    first_layer, top_layer = sec == 0, sec == sections - 1
    fetches = [
        (always, h_hbm, raw.at[0]), (always, c_hbm, flat.at[1]),
        (always, weight_hbm, weight), (always, bias_hbm, bias)]
    for t in range(frame_count):
        fetches.append((first_layer, frames.at[t], raw.at[1 + t]))
        fetches.append((top_layer, cotangent.at[t], raw.at[1 + frame_count + t]))
    fetches = [(cond, pltpu.make_async_copy(src, dst, fetched.at[k]))
               for k, (cond, src, dst) in enumerate(fetches)]
    for cond, fetch in fetches:
        pl.when(cond)(fetch.start)

    barrier = pltpu.get_barrier_semaphore()
    count = jnp.int32(m - 1 + n - 1)

    def greet(cond, device):
        @pl.when(cond)
        def _():
            pl.semaphore_signal(barrier, inc=1, device_id=device, device_id_type=MESH)
        return jnp.where(cond, 1, 0).astype(jnp.int32)

    for j in range(m):
        greet(tx != j, (sec, j, ty))
    for j in range(n):
        greet(ty != j, (sec, tx, j))
    for a, b in SIDES:
        if a and b:
            count = count + greet(present(a, b), (sec, tx + a, ty + b))
    for step in (-1, 1):
        there = (sec + step >= 0) & (sec + step < sections)
        for a, b in [(0, 0)] + SIDES:
            count = count + greet(there & present(a, b), (sec + step, tx + a, ty + b))

    x_set, h_set, u_set, g_set = 0, frame_count, 2 * frame_count, 3 * frame_count
    total[...] = jnp.zeros_like(total)
    pack[...] = jnp.zeros_like(pack)
    c_pack[...] = jnp.zeros_like(c_pack)
    at_row = lax.broadcasted_iota(jnp.int32, (16, cells), 0)
    at_lane = lax.broadcasted_iota(jnp.int32, (16, cells), 1)
    spot = jnp.where(at_row < rows, at_row * cols, (at_row - rows) * cols + cols - 1)
    pick[...] = jnp.where(at_lane == spot, 1.0, 0.0).astype(BF16)
    r16 = lax.broadcasted_iota(jnp.int32, (16, cells + 2 * cols), 0)
    at_lane = lax.broadcasted_iota(jnp.int32, (16, cells + 2 * cols), 1)
    for k in range(6):
        r = r16 - rows if k < 3 else r16
        inside = (r >= 0) & (r < rows)
        edge = 0 if k < 3 else cols - 1
        if k % 3 == 0:
            spot = jnp.where(r == rows - 1, edge, -1)
        elif k % 3 == 1:
            spot = jnp.where(inside, (r + 1) * cols + edge, -1)
        else:
            spot = jnp.where(r == 0, (rows + 1) * cols + edge, -1)
        place[pl.ds(16 * k, 16), :] = jnp.where(at_lane == spot, 1.0, 0.0).astype(BF16)

    for cond, fetch in fetches:
        pl.when(cond)(fetch.wait)

    def flatten(index, store):
        for r in range(rows):
            store(r, flat[index, pl.ds(r, width, stride=rows), :])

    def unpack(source, slot, dst):
        flat[slot] = raw[source].astype(F32)

        def store(r, value):
            dst[:, row_slice(r)] = value.astype(BF16)

        flatten(slot, store)

    def store_cell(r, value):
        cell[:, row_slice(r)] = value

    unpack(0, 0, h_init)
    flatten(1, store_cell)
    pack[h_set, :, 0:width] = packed(h_init[...])

    @pl.when(first_layer)
    def _():
        for t in range(frame_count):
            unpack(1 + t, 2 + t, x_in.at[t])
            pack[x_set + t, :, 0:width] = packed(x_in[t])

    @pl.when(top_layer)
    def _():
        for t in range(frame_count):
            unpack(1 + frame_count + t, 2 + t, dx_in.at[t])
            pack[u_set + t, :, 0:width] = packed(dx_in[t])

    for kr in range(3):
        wt[kr] = weight[kr * taps:(kr + 1) * taps, :].astype(F32).T.astype(BF16)
        for kc in range(3):
            k = kr * 3 + kc
            wb[2 - kr, :, (2 - kc) * gates:(3 - kc) * gates] = weight[k * 2 * width:(k + 1) * 2 * width, :]
    bcol[...] = jnp.broadcast_to(bias[...], (gates, gates)).T
    for ref in (dh_e, dh_s, dc_e, dc_s):
        ref[...] = jnp.zeros_like(ref)

    pl.semaphore_wait(barrier, count)

    first, last = row_slice(0), row_slice(rows - 1)

    def exchange(cond, target, tile, slot, to, event, rows_too=True):
        if rows_too:
            exchange_rows(cond, target, tile, to, event)
        send_sides(cond, target, None, None, pack.at[slot], row_in.at[to], col_in.at[to],
                   h_send.at[event], h_recv.at[to], range(2, 8))

    def exchange_rows(cond, target, tile, to, event):
        send_sides(cond, target, tile.at[:, first], tile.at[:, last], None, row_in.at[to],
                   col_in.at[to], h_send.at[event], h_recv.at[to], range(2))

    def need(t):
        return always if t else sec > 0

    def gathered(source, to):
        wait_sides(source, row_in.at[to], col_in.at[to], h_send.at[0], h_recv.at[to])

    extra = 4 * frame_count
    exchange(sec == 0, sec, x_in.at[0], x_set, x_set, x_set)
    exchange(always, sec, h_init, h_set, h_set, h_set)
    for t in range(1, frame_count):
        exchange(sec == 0, sec, x_in.at[t], x_set + t, x_set + t, x_set + t)
    for t in range(frame_count):
        exchange(top_layer & need(t), sec, dx_in.at[t], u_set + t, u_set + t, u_set + t)
    above = jnp.where(sec == sections - 1, sec, sec + 1)
    before_layer = jnp.where(sec == 0, sec, sec - 1)

    for t in range(frame_count):
        def store_z(offset, q):
            def store(kc, value):
                low = kc * 2 * width + offset
                zz[t, low:low + width, row_slice(q)] = value
            return store

        def fill(tile, to, offset):
            side = side_image(col_in[to], width)
            for q in range(rows + 2):
                if q == 0:
                    value = row_in[to, 0]
                elif q == rows + 1:
                    value = row_in[to, 1]
                else:
                    value = tile[:, row_slice(q - 1)]
                spread(value.astype(F32), side[:, q * cols:(q + 1) * cols], lane, store_z(offset, q))

        gathered(sec, h_set + t)
        fill(h_init if t == 0 else hidden.at[t - 1], h_set + t, width)
        arrive(sec > 0, x_in.at[t], x_send.at[t], x_recv.at[t], (before_layer, tx, ty))
        gathered(before_layer, x_set + t)
        fill(x_in.at[t], x_set + t, 0)

        act = jnp.zeros((gates, cells), F32)
        for kr in range(3):
            act = act + dot(wt[kr], zz[t, :, kr * cols:kr * cols + cells], ((1,), (0,)))
        column = bcol[...]
        for r in range(rows):
            at = row_slice(r)
            a = act[:, r * cols:(r + 1) * cols] + column
            gate_in = sigmoid(a[:width])
            gate_forget = sigmoid(a[width:2 * width])
            gate_out = sigmoid(a[2 * width:3 * width])
            gate_cell = jnp.tanh(a[3 * width:])
            before = cell[:, at]
            after = gate_forget * before + gate_in * gate_cell
            squash = jnp.tanh(after)
            cell[:, at] = after
            hidden[t, :, at] = (gate_out * squash).astype(BF16)
            for k, value in enumerate((
                    gate_cell * gate_in * (1.0 - gate_in),
                    before * gate_forget * (1.0 - gate_forget),
                    squash * gate_out * (1.0 - gate_out),
                    gate_in * (1.0 - gate_cell * gate_cell),
                    gate_out * (1.0 - squash * squash),
                    gate_forget)):
                coef[t, k, :, at] = value
                coef_b[t, k * width:(k + 1) * width, at] = value.astype(BF16)
        start(sec < sections - 1, hidden.at[t], x_in.at[t], x_send.at[t], x_recv.at[t],
              (sec + 1, tx, ty))
        exchange_rows(sec < sections - 1, sec + 1, hidden.at[t], x_set + t, extra + t)
        pack[extra + t, :, 0:width] = packed(hidden[t])
        exchange(sec < sections - 1, sec + 1, hidden.at[t], extra + t, x_set + t, extra + t, False)
        if t < frame_count - 1:
            exchange(always, sec, hidden.at[t], extra + t, h_set + t + 1, h_set + t + 1)
        c_pack[t, :, 0:6 * width] = packed(coef_b[t])
        send_sides(need(t), sec, coef_b.at[t, :, first], coef_b.at[t, :, last], c_pack.at[t],
                   c_row_in.at[t], c_col_in.at[t], c_send.at[t], c_recv.at[t])

    for t in reversed(range(frame_count)):
        def ring_ready():
            wait_sides(sec, c_row_in.at[t], c_col_in.at[t], c_send.at[t], c_recv.at[t])
            coef_s[...] = side_image(c_col_in[t], 6 * width)
            if t < frame_count - 1:
                gathered(sec, g_set + t + 1)
                dh_s[...] = side_image(col_in[g_set + t + 1], width)
                dh_e[:, row_slice(0)] = row_in[g_set + t + 1, 0].astype(F32)
                dh_e[:, row_slice(rows + 1)] = row_in[g_set + t + 1, 1].astype(F32)

        def gate_grads(u, dh_ref, dc_ref, at, k_of):
            dh = u + dh_ref[:, at]
            dc = dc_ref[:, at] + dh * k_of(4)
            if t:
                dc_ref[:, at] = dc * k_of(5)
            return jnp.concatenate([dc * k_of(0), dc * k_of(1), dh * k_of(2), dc * k_of(3)], 0)

        def input_grad():
            gathered(above, u_set + t)
            u_s = side_image(col_in[u_set + t], width)
            for q in range(rows + 2):
                at = row_slice(q)
                if 0 < q <= rows:
                    main = da[t, :, row_slice(q - 1)].astype(F32)
                else:
                    end = 0 if q == 0 else 1
                    main = gate_grads(
                        row_in[u_set + t, end].astype(F32), dh_e, dc_e, at,
                        lambda k: c_row_in[t, end, k * width:(k + 1) * width, :].astype(F32))
                side = gate_grads(u_s[:, q * cols:(q + 1) * cols], dh_s, dc_s, at,
                                  lambda k: coef_s[k * width:(k + 1) * width, at])

                def store_d(kc, value):
                    dd[kc * gates:(kc + 1) * gates, at] = value

                spread(main, side, lane_d, store_d)
            dz = jnp.zeros((2 * width, cells), F32)
            for kr in range(3):
                dz = dz + dot(wb[kr], dd[:, kr * cols:kr * cols + cells], ((1,), (0,)))
            dx_out[t] = dz[:width].astype(BF16)
            if t:
                dh_out[t] = dz[width:].astype(BF16)
                dh_e[:, pl.ds(cols, cells)] = dz[width:]

        def when_needed(work):
            if t:
                work()
            else:
                pl.when(sec > 0)(work)

        when_needed(ring_ready)
        arrive(sec < sections - 1, dx_in.at[t], u_send.at[t], u_recv.at[t], (above, tx, ty))
        for r in range(rows):
            main = gate_grads(dx_in[t, :, row_slice(r)].astype(F32), dh_e, dc_e, row_slice(r + 1),
                              lambda k: coef[t, k, :, row_slice(r)])
            da[t, :, row_slice(r)] = main.astype(BF16)
        when_needed(input_grad)
        start(sec > 0, dx_out.at[t], dx_in.at[t], u_send.at[t], u_recv.at[t], (sec - 1, tx, ty))
        below = sec > 0 if t else sec > 1
        slot = extra + frame_count + t
        exchange_rows(below, sec - 1, dx_out.at[t], u_set + t, slot)

        @pl.when(below)
        def _():
            pack[slot, :, 0:width] = packed(dx_out[t])

        exchange(below, sec - 1, dx_out.at[t], slot, u_set + t, slot, False)
        if t:
            pack[g_set + t, :, 0:width] = packed(dh_out[t])
            exchange(need(t - 1), sec, dh_out.at[t], g_set + t, g_set + t, g_set + t)
        for kr in range(3):
            at = pl.ds(kr * taps, taps)
            total[at, :] += dot(zz[t, :, kr * cols:kr * cols + cells], da[t], ((1,), (1,)))
        total[pl.ds(3 * taps, 8), :] += dot(jnp.ones((8, cells), BF16), da[t], ((1,), (1,)))

    c1 = total.shape[0] // n
    c2 = c1 // m
    for j in range(n):
        start(ty != j, total.at[pl.ds(j * c1, c1)], recv1.at[ty], s1.at[j], r1.at[ty], (sec, tx, j))
    mine1 = pl.ds(pl.multiple_of(ty * c1, 16), c1)
    part1[...] = total[mine1, :]
    for j in range(n):
        arrive(ty != j, recv1.at[j], s1.at[j], r1.at[j], (sec, tx, j))

        @pl.when(ty != j)
        def _():
            part1[...] += recv1[j]
    for j in range(m):
        start(tx != j, part1.at[pl.ds(j * c2, c2)], recv2.at[tx], s2.at[j], r2.at[tx], (sec, j, ty))
    mine2 = pl.ds(pl.multiple_of(tx * c2, 16), c2)
    for j in range(m):
        arrive(tx != j, recv2.at[j], s2.at[j], r2.at[j], (sec, j, ty))

        @pl.when(tx != j)
        def _():
            part1[mine2, :] += recv2[j]
    own = pl.ds(pl.multiple_of(ty * c1 + tx * c2, 16), c2)
    done[own, :] = part1[mine2, :].astype(BF16)
    for j in range(m):
        start(tx != j, done.at[own], done.at[own], s3.at[j], r3.at[tx], (sec, j, ty))
    for j in range(m):
        theirs = pl.ds(pl.multiple_of(ty * c1 + j * c2, 16), c2)
        arrive(tx != j, done.at[theirs], s3.at[j], r3.at[j], (sec, j, ty))
    for j in range(n):
        start(ty != j, done.at[mine1], done.at[mine1], s4.at[j], r4.at[ty], (sec, tx, j))
    for j in range(n):
        arrive(ty != j, done.at[pl.ds(j * c1, c1)], s4.at[j], r4.at[j], (sec, tx, j))
    grad_w[...] = done[pl.ds(0, 3 * taps), :].astype(F32)
    grad_b[...] = done[pl.ds(3 * taps, 16), :].astype(F32)[0:1]

    for cond, make in pending:
        pl.when(cond)(lambda make=make: make().wait_send())


def body(dims, frames, h_init, c_init, weights, biases, cotangent):
    sections, m, n = dims
    frame_count, width, row_count, col_count = frames.shape
    cells = row_count * col_count
    ext = cells + 2 * col_count
    gates = 4 * width
    taps = weights.shape[1] // 3
    unit = m * n * 16
    tall = -(-(3 * taps + 8) // unit) * unit
    c1 = tall // n
    c2 = c1 // m
    vmem = pl.BlockSpec(memory_space=pltpu.VMEM)
    hbm = pl.BlockSpec(memory_space=pl.ANY)
    dma = pltpu.SemaphoreType.DMA
    f = frame_count
    spread_rows = width * row_count
    scratch = [
        pltpu.VMEM((3 * taps, gates), BF16),
        pltpu.VMEM((1, gates), F32),
        pltpu.VMEM((1 + 2 * f, spread_rows, col_count), BF16),
        pltpu.VMEM((2 + f, spread_rows, col_count), F32),
        pltpu.VMEM((width, cells), BF16),
        pltpu.VMEM((3, gates, taps), BF16),
        pltpu.VMEM((3, 2 * width, 3 * gates), BF16),
        pltpu.VMEM((gates, gates), F32),
        pltpu.VMEM((16, cells), BF16),
        pltpu.VMEM((6 * 16, ext), BF16),
        pltpu.VMEM((f, taps, ext), BF16),
        pltpu.VMEM((3 * gates, ext), BF16),
        pltpu.VMEM((f, 6, width, cells), F32),
        pltpu.VMEM((f, 6 * width, cells), BF16),
        pltpu.VMEM((6 * width, ext), F32),
        pltpu.VMEM((width, cells), F32),
        pltpu.VMEM((f, width, cells), BF16),
        pltpu.VMEM((f, width, cells), BF16),
        pltpu.VMEM((f, width, cells), BF16),
        pltpu.VMEM((f, width, cells), BF16),
        pltpu.VMEM((f, gates, cells), BF16),
        pltpu.VMEM((width, ext), F32),
        pltpu.VMEM((width, ext), F32),
        pltpu.VMEM((width, ext), F32),
        pltpu.VMEM((width, ext), F32),
        pltpu.VMEM((6 * f, 16, col_count), BF16),
        pltpu.VMEM((4 * f, 2, width, col_count), BF16),
        pltpu.VMEM((4 * f, 6, 16, col_count), BF16),
        pltpu.VMEM((f, 16, 2 * col_count), BF16),
        pltpu.VMEM((f, 2, 6 * width, col_count), BF16),
        pltpu.VMEM((f, 6, 16, 2 * col_count), BF16),
        pltpu.VMEM((tall, gates), F32),
        pltpu.VMEM((n, c1, gates), F32),
        pltpu.VMEM((c1, gates), F32),
        pltpu.VMEM((m, c2, gates), F32),
        pltpu.VMEM((tall, gates), BF16),
        dma((6 * f, 8)), dma((4 * f, 8)),
        dma((f,)), dma((f,)),
        dma((f, 8)), dma((f, 8)),
        dma((f,)), dma((f,)),
        dma((n,)), dma((n,)), dma((m,)), dma((m,)),
        dma((m,)), dma((m,)), dma((n,)), dma((n,)),
        dma((4 + 2 * f,)),
    ]
    hidden, grad_w, grad_b = pl.pallas_call(
        functools.partial(kernel, dims),
        out_shape=(
            jax.ShapeDtypeStruct((f, width, cells), BF16),
            jax.ShapeDtypeStruct((3 * taps, gates), F32),
            jax.ShapeDtypeStruct((1, gates), F32),
        ),
        in_specs=[hbm] * 6,
        out_specs=(vmem, vmem, vmem),
        scratch_shapes=scratch,
        compiler_params=pltpu.CompilerParams(
            collective_id=0, has_side_effects=True, vmem_limit_bytes=48 * 1024 * 1024),
    )(
        frames.reshape(f, spread_rows, col_count),
        h_init.reshape(spread_rows, col_count),
        c_init.reshape(spread_rows, col_count),
        weights[0],
        biases,
        cotangent.reshape(f, spread_rows, col_count),
    )
    return (hidden.reshape(1, f, width, row_count, col_count), grad_w[None], grad_b)


def solution(mesh):
    dims = (mesh.shape["section"], mesh.shape["tx"], mesh.shape["ty"])
    in_specs = (
        P(None, None, "tx", "ty"),
        P("section", None, "tx", "ty"),
        P("section", None, "tx", "ty"),
        P("section", None, None),
        P("section", None),
        P(None, None, "tx", "ty"),
    )
    out_specs = (P("section", None, None, "tx", "ty"), P("section", None, None), P("section", None))
    return jax.shard_map(functools.partial(body, dims), mesh=mesh, in_specs=in_specs,
                         out_specs=out_specs, check_vma=False)
```

```python
import functools

import jax
import jax.numpy as jnp
from jax import lax
from jax.experimental import pallas as pl
from jax.experimental.pallas import tpu as pltpu
from jax.sharding import PartitionSpec as P

MESH = pl.DeviceIdType.MESH
SIDES = [(-1, 0), (1, 0), (-1, -1), (0, -1), (1, -1), (-1, 1), (0, 1), (1, 1)]
SLOT = {side: index for index, side in enumerate(SIDES)}
F32 = jnp.float32
BF16 = jnp.bfloat16


def sigmoid(x):
    return 0.5 * jnp.tanh(0.5 * x) + 0.5


def dot(x, y, contract):
    return lax.dot_general(x, y, (contract, ((), ())), preferred_element_type=F32)


def kernel(dims, frames, h_hbm, c_hbm, weight_hbm, bias_hbm, cotangent, hidden, grad_w, grad_b,
           weight, bias, raw, flat, h_init, wt, wb, bcol, pick, place, zz, dd, coef, coef_b, coef_s, cell, x_in, dx_in, dx_out, dh_out, da,
           dh_e, dh_s, dc_e, dc_s, pack, row_in, col_in, c_pack, c_row_in, c_col_in,
           total, recv1, part1, recv2, done,
           h_send, h_recv, x_send, x_recv, c_send, c_recv, u_send, u_recv,
           s1, r1, s2, r2, s3, r3, s4, r4, fetched):
    sections, m, n = dims
    frame_count, width, cells = hidden.shape
    cols = frames.shape[2]
    rows = cells // cols
    gates = 4 * width
    taps = weight.shape[0] // 3
    sec = lax.axis_index("section")
    tx = lax.axis_index("tx")
    ty = lax.axis_index("ty")
    pending = []
    always = jnp.bool_(True)

    def present(a, b):
        ok = always
        if a:
            ok = ok & (tx + a >= 0) & (tx + a < m)
        if b:
            ok = ok & (ty + b >= 0) & (ty + b < n)
        return ok

    def start(cond, src, dst, send_sem, recv_sem, device):
        def make():
            return pltpu.make_async_remote_copy(
                src_ref=src, dst_ref=dst, send_sem=send_sem, recv_sem=recv_sem,
                device_id=device, device_id_type=MESH)

        @pl.when(cond)
        def _():
            make().start()

        pending.append((cond, make))

    def arrive(cond, dst, send_sem, recv_sem, device):
        @pl.when(cond)
        def _():
            pltpu.make_async_remote_copy(
                src_ref=dst, dst_ref=dst, send_sem=send_sem, recv_sem=recv_sem,
                device_id=device, device_id_type=MESH).wait_recv()

    def landing(rows_ref, cols_ref, slot):
        return rows_ref.at[slot] if slot < 2 else cols_ref.at[slot - 2]

    def send_sides(cond, target, first, last, packed, rows_ref, cols_ref, send_sems, recv_sems,
                   which=range(8)):
        for d in which:
            a, b = SIDES[d]
            src = packed if b else (first if a < 0 else last)
            slot = SLOT[(-a, -b)]
            start(cond & present(a, b), src, landing(rows_ref, cols_ref, slot), send_sems.at[d],
                  recv_sems.at[slot], (target, tx + a, ty + b))

    def wait_sides(source, rows_ref, cols_ref, send_sems, recv_sems):
        for d, (a, b) in enumerate(SIDES):
            arrive(present(a, b), landing(rows_ref, cols_ref, d), send_sems.at[d], recv_sems.at[d],
                   (source, tx + a, ty + b))

    def packed(tile):
        return dot(pick[...], tile, ((1,), (1,))).astype(BF16)

    def side_image(slots, height):
        return dot(slots.reshape(6 * 16, slots.shape[2])[:, :height], place[...], ((0,), (0,)))

    def row_slice(r):
        return pl.ds(r * cols, cols)

    lane = lax.broadcasted_iota(jnp.int32, (width, cols), 1)
    lane_d = lax.broadcasted_iota(jnp.int32, (gates, cols), 1)

    def spread(value, side, lanes, store):
        low = jnp.where(lanes == 0, side, pltpu.roll(value, 1, 1))
        high = jnp.where(lanes == cols - 1, side, pltpu.roll(value, cols - 1, 1))
        store(0, low.astype(BF16))
        store(1, value.astype(BF16))
        store(2, high.astype(BF16))

    row_in[...] = jnp.zeros_like(row_in)
    col_in[...] = jnp.zeros_like(col_in)
    c_row_in[...] = jnp.zeros_like(c_row_in)
    c_col_in[...] = jnp.zeros_like(c_col_in)

    first_layer, top_layer = sec == 0, sec == sections - 1
    fetches = [
        (always, h_hbm, raw.at[0]), (always, c_hbm, flat.at[1]),
        (always, weight_hbm, weight), (always, bias_hbm, bias)]
    for t in range(frame_count):
        fetches.append((first_layer, frames.at[t], raw.at[1 + t]))
        fetches.append((top_layer, cotangent.at[t], raw.at[1 + frame_count + t]))
    fetches = [(cond, pltpu.make_async_copy(src, dst, fetched.at[k]))
               for k, (cond, src, dst) in enumerate(fetches)]
    for cond, fetch in fetches:
        pl.when(cond)(fetch.start)

    barrier = pltpu.get_barrier_semaphore()
    count = jnp.int32(m - 1 + n - 1)

    def greet(cond, device):
        @pl.when(cond)
        def _():
            pl.semaphore_signal(barrier, inc=1, device_id=device, device_id_type=MESH)
        return jnp.where(cond, 1, 0).astype(jnp.int32)

    for j in range(m):
        greet(tx != j, (sec, j, ty))
    for j in range(n):
        greet(ty != j, (sec, tx, j))
    for a, b in SIDES:
        if a and b:
            count = count + greet(present(a, b), (sec, tx + a, ty + b))
    for step in (-1, 1):
        there = (sec + step >= 0) & (sec + step < sections)
        for a, b in [(0, 0)] + SIDES:
            count = count + greet(there & present(a, b), (sec + step, tx + a, ty + b))

    x_set, h_set, u_set, g_set = 0, frame_count, 2 * frame_count, 3 * frame_count
    total[...] = jnp.zeros_like(total)
    pack[...] = jnp.zeros_like(pack)
    c_pack[...] = jnp.zeros_like(c_pack)
    at_row = lax.broadcasted_iota(jnp.int32, (16, cells), 0)
    at_lane = lax.broadcasted_iota(jnp.int32, (16, cells), 1)
    spot = jnp.where(at_row < rows, at_row * cols, (at_row - rows) * cols + cols - 1)
    pick[...] = jnp.where(at_lane == spot, 1.0, 0.0).astype(BF16)
    r16 = lax.broadcasted_iota(jnp.int32, (16, cells + 2 * cols), 0)
    at_lane = lax.broadcasted_iota(jnp.int32, (16, cells + 2 * cols), 1)
    for k in range(6):
        r = r16 - rows if k < 3 else r16
        inside = (r >= 0) & (r < rows)
        edge = 0 if k < 3 else cols - 1
        if k % 3 == 0:
            spot = jnp.where(r == rows - 1, edge, -1)
        elif k % 3 == 1:
            spot = jnp.where(inside, (r + 1) * cols + edge, -1)
        else:
            spot = jnp.where(r == 0, (rows + 1) * cols + edge, -1)
        place[pl.ds(16 * k, 16), :] = jnp.where(at_lane == spot, 1.0, 0.0).astype(BF16)

    for cond, fetch in fetches:
        pl.when(cond)(fetch.wait)

    def flatten(index, store):
        for r in range(rows):
            store(r, flat[index, pl.ds(r, width, stride=rows), :])

    def unpack(source, slot, dst):
        flat[slot] = raw[source].astype(F32)

        def store(r, value):
            dst[:, row_slice(r)] = value.astype(BF16)

        flatten(slot, store)

    def store_cell(r, value):
        cell[:, row_slice(r)] = value

    unpack(0, 0, h_init)
    flatten(1, store_cell)
    pack[h_set, :, 0:width] = packed(h_init[...])

    @pl.when(first_layer)
    def _():
        for t in range(frame_count):
            unpack(1 + t, 2 + t, x_in.at[t])
            pack[x_set + t, :, 0:width] = packed(x_in[t])

    @pl.when(top_layer)
    def _():
        for t in range(frame_count):
            unpack(1 + frame_count + t, 2 + t, dx_in.at[t])
            pack[u_set + t, :, 0:width] = packed(dx_in[t])

    for kr in range(3):
        wt[kr] = weight[kr * taps:(kr + 1) * taps, :].astype(F32).T.astype(BF16)
        for kc in range(3):
            k = kr * 3 + kc
            wb[2 - kr, :, (2 - kc) * gates:(3 - kc) * gates] = weight[k * 2 * width:(k + 1) * 2 * width, :]
    bcol[...] = jnp.broadcast_to(bias[...], (gates, gates)).T
    for ref in (dh_e, dh_s, dc_e, dc_s):
        ref[...] = jnp.zeros_like(ref)

    pl.semaphore_wait(barrier, count)

    first, last = row_slice(0), row_slice(rows - 1)

    def exchange(cond, target, tile, slot, to, event, rows_too=True):
        if rows_too:
            exchange_rows(cond, target, tile, to, event)
        send_sides(cond, target, None, None, pack.at[slot], row_in.at[to], col_in.at[to],
                   h_send.at[event], h_recv.at[to], range(2, 8))

    def exchange_rows(cond, target, tile, to, event):
        send_sides(cond, target, tile.at[:, first], tile.at[:, last], None, row_in.at[to],
                   col_in.at[to], h_send.at[event], h_recv.at[to], range(2))

    def need(t):
        return always if t else sec > 0

    def gathered(source, to):
        wait_sides(source, row_in.at[to], col_in.at[to], h_send.at[0], h_recv.at[to])

    extra = 4 * frame_count
    exchange(sec == 0, sec, x_in.at[0], x_set, x_set, x_set)
    exchange(always, sec, h_init, h_set, h_set, h_set)
    for t in range(1, frame_count):
        exchange(sec == 0, sec, x_in.at[t], x_set + t, x_set + t, x_set + t)
    for t in range(frame_count):
        exchange(top_layer & need(t), sec, dx_in.at[t], u_set + t, u_set + t, u_set + t)
    above = jnp.where(sec == sections - 1, sec, sec + 1)
    before_layer = jnp.where(sec == 0, sec, sec - 1)

    for t in range(frame_count):
        def store_z(offset, q):
            def store(kc, value):
                low = kc * 2 * width + offset
                zz[t, low:low + width, row_slice(q)] = value
            return store

        def fill(tile, to, offset):
            side = side_image(col_in[to], width)
            for q in range(rows + 2):
                if q == 0:
                    value = row_in[to, 0]
                elif q == rows + 1:
                    value = row_in[to, 1]
                else:
                    value = tile[:, row_slice(q - 1)]
                spread(value.astype(F32), side[:, q * cols:(q + 1) * cols], lane, store_z(offset, q))

        gathered(sec, h_set + t)
        fill(h_init if t == 0 else hidden.at[t - 1], h_set + t, width)
        arrive(sec > 0, x_in.at[t], x_send.at[t], x_recv.at[t], (before_layer, tx, ty))
        gathered(before_layer, x_set + t)
        fill(x_in.at[t], x_set + t, 0)

        act = jnp.zeros((gates, cells), F32)
        for kr in range(3):
            act = act + dot(wt[kr], zz[t, :, kr * cols:kr * cols + cells], ((1,), (0,)))
        column = bcol[...]
        for r in range(rows):
            at = row_slice(r)
            a = act[:, r * cols:(r + 1) * cols] + column
            gate_in = sigmoid(a[:width])
            gate_forget = sigmoid(a[width:2 * width])
            gate_out = sigmoid(a[2 * width:3 * width])
            gate_cell = jnp.tanh(a[3 * width:])
            before = cell[:, at]
            after = gate_forget * before + gate_in * gate_cell
            squash = jnp.tanh(after)
            cell[:, at] = after
            hidden[t, :, at] = (gate_out * squash).astype(BF16)
            for k, value in enumerate((
                    gate_cell * gate_in * (1.0 - gate_in),
                    before * gate_forget * (1.0 - gate_forget),
                    squash * gate_out * (1.0 - gate_out),
                    gate_in * (1.0 - gate_cell * gate_cell),
                    gate_out * (1.0 - squash * squash),
                    gate_forget)):
                coef[t, k, :, at] = value
                coef_b[t, k * width:(k + 1) * width, at] = value.astype(BF16)
        start(sec < sections - 1, hidden.at[t], x_in.at[t], x_send.at[t], x_recv.at[t],
              (sec + 1, tx, ty))
        exchange_rows(sec < sections - 1, sec + 1, hidden.at[t], x_set + t, extra + t)
        pack[extra + t, :, 0:width] = packed(hidden[t])
        exchange(sec < sections - 1, sec + 1, hidden.at[t], extra + t, x_set + t, extra + t, False)
        if t < frame_count - 1:
            exchange(always, sec, hidden.at[t], extra + t, h_set + t + 1, h_set + t + 1)
        c_pack[t, :, 0:6 * width] = packed(coef_b[t])
        send_sides(need(t), sec, coef_b.at[t, :, first], coef_b.at[t, :, last], c_pack.at[t],
                   c_row_in.at[t], c_col_in.at[t], c_send.at[t], c_recv.at[t])

    for t in reversed(range(frame_count)):
        def ring_ready():
            wait_sides(sec, c_row_in.at[t], c_col_in.at[t], c_send.at[t], c_recv.at[t])
            coef_s[...] = side_image(c_col_in[t], 6 * width)
            if t < frame_count - 1:
                gathered(sec, g_set + t + 1)
                dh_s[...] = side_image(col_in[g_set + t + 1], width)
                dh_e[:, row_slice(0)] = row_in[g_set + t + 1, 0].astype(F32)
                dh_e[:, row_slice(rows + 1)] = row_in[g_set + t + 1, 1].astype(F32)

        def gate_grads(u, dh_ref, dc_ref, at, k_of):
            dh = u + dh_ref[:, at]
            dc = dc_ref[:, at] + dh * k_of(4)
            if t:
                dc_ref[:, at] = dc * k_of(5)
            return jnp.concatenate([dc * k_of(0), dc * k_of(1), dh * k_of(2), dc * k_of(3)], 0)

        def input_grad():
            gathered(above, u_set + t)
            u_s = side_image(col_in[u_set + t], width)
            for q in range(rows + 2):
                at = row_slice(q)
                if 0 < q <= rows:
                    main = da[t, :, row_slice(q - 1)].astype(F32)
                else:
                    end = 0 if q == 0 else 1
                    main = gate_grads(
                        row_in[u_set + t, end].astype(F32), dh_e, dc_e, at,
                        lambda k: c_row_in[t, end, k * width:(k + 1) * width, :].astype(F32))
                side = gate_grads(u_s[:, q * cols:(q + 1) * cols], dh_s, dc_s, at,
                                  lambda k: coef_s[k * width:(k + 1) * width, at])

                def store_d(kc, value):
                    dd[kc * gates:(kc + 1) * gates, at] = value

                spread(main, side, lane_d, store_d)
            dz = jnp.zeros((2 * width, cells), F32)
            for kr in range(3):
                dz = dz + dot(wb[kr], dd[:, kr * cols:kr * cols + cells], ((1,), (0,)))
            dx_out[t] = dz[:width].astype(BF16)
            if t:
                dh_out[t] = dz[width:].astype(BF16)
                dh_e[:, pl.ds(cols, cells)] = dz[width:]

        def when_needed(work):
            if t:
                work()
            else:
                pl.when(sec > 0)(work)

        when_needed(ring_ready)
        arrive(sec < sections - 1, dx_in.at[t], u_send.at[t], u_recv.at[t], (above, tx, ty))
        for r in range(rows):
            main = gate_grads(dx_in[t, :, row_slice(r)].astype(F32), dh_e, dc_e, row_slice(r + 1),
                              lambda k: coef[t, k, :, row_slice(r)])
            da[t, :, row_slice(r)] = main.astype(BF16)
        when_needed(input_grad)
        start(sec > 0, dx_out.at[t], dx_in.at[t], u_send.at[t], u_recv.at[t], (sec - 1, tx, ty))
        below = sec > 0 if t else sec > 1
        slot = extra + frame_count + t
        exchange_rows(below, sec - 1, dx_out.at[t], u_set + t, slot)

        @pl.when(below)
        def _():
            pack[slot, :, 0:width] = packed(dx_out[t])

        exchange(below, sec - 1, dx_out.at[t], slot, u_set + t, slot, False)
        if t:
            pack[g_set + t, :, 0:width] = packed(dh_out[t])
            exchange(need(t - 1), sec, dh_out.at[t], g_set + t, g_set + t, g_set + t)
        for kr in range(3):
            at = pl.ds(kr * taps, taps)
            total[at, :] += dot(zz[t, :, kr * cols:kr * cols + cells], da[t], ((1,), (1,)))
        total[pl.ds(3 * taps, 8), :] += dot(jnp.ones((8, cells), BF16), da[t], ((1,), (1,)))

    c1 = total.shape[0] // n
    c2 = c1 // m
    for j in range(n):
        start(ty != j, total.at[pl.ds(j * c1, c1)], recv1.at[ty], s1.at[j], r1.at[ty], (sec, tx, j))
    mine1 = pl.ds(pl.multiple_of(ty * c1, 16), c1)
    part1[...] = total[mine1, :]
    for j in range(n):
        arrive(ty != j, recv1.at[j], s1.at[j], r1.at[j], (sec, tx, j))

        @pl.when(ty != j)
        def _():
            part1[...] += recv1[j]
    for j in range(m):
        start(tx != j, part1.at[pl.ds(j * c2, c2)], recv2.at[tx], s2.at[j], r2.at[tx], (sec, j, ty))
    mine2 = pl.ds(pl.multiple_of(tx * c2, 16), c2)
    for j in range(m):
        arrive(tx != j, recv2.at[j], s2.at[j], r2.at[j], (sec, j, ty))

        @pl.when(tx != j)
        def _():
            part1[mine2, :] += recv2[j]
    own = pl.ds(pl.multiple_of(ty * c1 + tx * c2, 16), c2)
    done[own, :] = part1[mine2, :].astype(BF16)
    for j in range(m):
        start(tx != j, done.at[own], done.at[own], s3.at[j], r3.at[tx], (sec, j, ty))
    for j in range(m):
        theirs = pl.ds(pl.multiple_of(ty * c1 + j * c2, 16), c2)
        arrive(tx != j, done.at[theirs], s3.at[j], r3.at[j], (sec, j, ty))
    for j in range(n):
        start(ty != j, done.at[mine1], done.at[mine1], s4.at[j], r4.at[ty], (sec, tx, j))
    for j in range(n):
        arrive(ty != j, done.at[pl.ds(j * c1, c1)], s4.at[j], r4.at[j], (sec, tx, j))
    grad_w[...] = done[pl.ds(0, 3 * taps), :].astype(F32)
    grad_b[...] = done[pl.ds(3 * taps, 16), :].astype(F32)[0:1]

    for cond, make in pending:
        pl.when(cond)(lambda make=make: make().wait_send())


def body(dims, frames, h_init, c_init, weights, biases, cotangent):
    sections, m, n = dims
    frame_count, width, row_count, col_count = frames.shape
    cells = row_count * col_count
    ext = cells + 2 * col_count
    gates = 4 * width
    taps = weights.shape[1] // 3
    unit = m * n * 16
    tall = -(-(3 * taps + 8) // unit) * unit
    c1 = tall // n
    c2 = c1 // m
    vmem = pl.BlockSpec(memory_space=pltpu.VMEM)
    hbm = pl.BlockSpec(memory_space=pltpu.HBM)
    dma = pltpu.SemaphoreType.DMA
    f = frame_count
    spread_rows = width * row_count
    scratch = [
        pltpu.VMEM((3 * taps, gates), BF16),
        pltpu.VMEM((1, gates), F32),
        pltpu.VMEM((1 + 2 * f, spread_rows, col_count), BF16),
        pltpu.VMEM((2 + f, spread_rows, col_count), F32),
        pltpu.VMEM((width, cells), BF16),
        pltpu.VMEM((3, gates, taps), BF16),
        pltpu.VMEM((3, 2 * width, 3 * gates), BF16),
        pltpu.VMEM((gates, gates), F32),
        pltpu.VMEM((16, cells), BF16),
        pltpu.VMEM((6 * 16, ext), BF16),
        pltpu.VMEM((f, taps, ext), BF16),
        pltpu.VMEM((3 * gates, ext), BF16),
        pltpu.VMEM((f, 6, width, cells), F32),
        pltpu.VMEM((f, 6 * width, cells), BF16),
        pltpu.VMEM((6 * width, ext), F32),
        pltpu.VMEM((width, cells), F32),
        pltpu.VMEM((f, width, cells), BF16),
        pltpu.VMEM((f, width, cells), BF16),
        pltpu.VMEM((f, width, cells), BF16),
        pltpu.VMEM((f, width, cells), BF16),
        pltpu.VMEM((f, gates, cells), BF16),
        pltpu.VMEM((width, ext), F32),
        pltpu.VMEM((width, ext), F32),
        pltpu.VMEM((width, ext), F32),
        pltpu.VMEM((width, ext), F32),
        pltpu.VMEM((6 * f, 16, col_count), BF16),
        pltpu.VMEM((4 * f, 2, width, col_count), BF16),
        pltpu.VMEM((4 * f, 6, 16, col_count), BF16),
        pltpu.VMEM((f, 16, 2 * col_count), BF16),
        pltpu.VMEM((f, 2, 6 * width, col_count), BF16),
        pltpu.VMEM((f, 6, 16, 2 * col_count), BF16),
        pltpu.VMEM((tall, gates), F32),
        pltpu.VMEM((n, c1, gates), F32),
        pltpu.VMEM((c1, gates), F32),
        pltpu.VMEM((m, c2, gates), F32),
        pltpu.VMEM((tall, gates), BF16),
        dma((6 * f, 8)), dma((4 * f, 8)),
        dma((f,)), dma((f,)),
        dma((f, 8)), dma((f, 8)),
        dma((f,)), dma((f,)),
        dma((n,)), dma((n,)), dma((m,)), dma((m,)),
        dma((m,)), dma((m,)), dma((n,)), dma((n,)),
        dma((4 + 2 * f,)),
    ]
    hidden, grad_w, grad_b = pl.pallas_call(
        functools.partial(kernel, dims),
        out_shape=(
            jax.ShapeDtypeStruct((f, width, cells), BF16),
            jax.ShapeDtypeStruct((3 * taps, gates), F32),
            jax.ShapeDtypeStruct((1, gates), F32),
        ),
        in_specs=[hbm] * 6,
        out_specs=(vmem, vmem, vmem),
        scratch_shapes=scratch,
        compiler_params=pltpu.CompilerParams(
            collective_id=0, has_side_effects=True, vmem_limit_bytes=63 * 1024 * 1024),
    )(
        frames.reshape(f, spread_rows, col_count),
        h_init.reshape(spread_rows, col_count),
        c_init.reshape(spread_rows, col_count),
        weights[0],
        biases,
        cotangent.reshape(f, spread_rows, col_count),
    )
    return (hidden.reshape(1, f, width, row_count, col_count), grad_w[None], grad_b)


def solution(mesh):
    dims = (mesh.shape["section"], mesh.shape["tx"], mesh.shape["ty"])
    in_specs = (
        P(None, None, "tx", "ty"),
        P("section", None, "tx", "ty"),
        P("section", None, "tx", "ty"),
        P("section", None, None),
        P("section", None),
        P(None, None, "tx", "ty"),
    )
    out_specs = (P("section", None, None, "tx", "ty"), P("section", None, None), P("section", None))
    return jax.shard_map(functools.partial(body, dims), mesh=mesh, in_specs=in_specs,
                         out_specs=out_specs, check_vma=False)
```
